32 devices in a mesh: ta: 16 (over z, x, core), row: 2 (over y).
Axes of the slice: x: 2, y: 2, z: 4, core: 2. Of those that a mesh axis runs over, the one named last changes fastest.
Arguments:
- amplitudes: float32 [8, 512, 96, 512], P(None, 'ta', 'row'), may hold values from -6 to 6
- integrals: bfloat16 [96, 512, 4, 512], P('row', 'ta'), may hold values from -0.0390625 to 0.0390625
Outputs:
- cycle: float32 [8, 512, 4, 512], P(None, 'row', None, 'ta')
The draws below stay inside these ranges and needn't reach their ends.
All inputs are finite; a program needn't handle non-finite values.
Results may differ from the reference program's by a relative error of at most 0.0029.
Values may be sent and summed in bfloat16 or wider, within the bound.
No kernel may reach another device: no remote copies, remote signals or barrier semaphores. Data moves between devices by JAX's collectives and lax.ppermute only.
A program may use at most 256 MiB of HBM per device.

```python
import jax
import jax.numpy as jnp
from jax import lax

VIRTUAL = 512
OCCUPIED = 96
J_SLAB = 4
I_SLAB = 8


def strengthened(entries, rng, source, target, shards_of, factor):
    def block_of(dim):
        return (jnp.arange(entries.shape[dim]) // (entries.shape[dim] // shards_of)).reshape((-1,) + (1,) * (entries.ndim - 1 - dim))

    one_side = jax.random.permutation(rng, shards_of)[block_of(target)]
    far = (block_of(target) + shards_of // 2) % shards_of
    return jnp.where((block_of(source) == one_side) | (block_of(source) == far), factor * entries, entries)


def levels(key, shape, shards, smallest, top_value):
    loudness = 1.0
    for position, parts in shards:
        draws = jax.random.uniform(jax.random.fold_in(jax.random.fold_in(key, 6), position), (parts,), jnp.float32, smallest / len(shards), top_value / len(shards))
        loudness = loudness * jnp.repeat(jnp.exp(draws), shape[position] // parts).reshape((-1,) + (1,) * (len(shape) - 1 - position))
    return loudness


def normal_values(stream_key, dims, width, reach, shards=(), dtype=jnp.bfloat16):
    values = jax.random.normal(stream_key, dims, jnp.float32) * width
    if len(shards) > 0:
        values = levels(stream_key, dims, shards, -0.22, 0.18) * values
    return jnp.clip(values, min=-reach, max=reach).astype(dtype)


def heavy_noise(own_key, shape, scale, bound, shards, heavy, kind=jnp.bfloat16):
    result = scale * jax.random.normal(own_key, shape, jnp.float32)
    if shards:
        result = result * levels(own_key, shape, shards, -0.22, 0.18)
    return jnp.clip(strengthened(result, jax.random.fold_in(own_key, 3), *heavy), -bound, bound).astype(kind)


def setup_inputs(seed: int = 0) -> dict:
    arg_keys = jax.random.split(jax.random.key(seed), 3)
    amplitudes = normal_values(arg_keys[0], (I_SLAB, VIRTUAL, OCCUPIED, VIRTUAL), 1.0, 6.0, ((1, 16), (2, 2)), jnp.float32)
    integrals = heavy_noise(arg_keys[1], (OCCUPIED, VIRTUAL, J_SLAB, VIRTUAL), (OCCUPIED * VIRTUAL) ** -0.5, 0.0390625, ((0, 2), (1, 16)), (1, 3, 16, 2.0))
    return dict(amplitudes=amplitudes, integrals=integrals)


def reference(amplitudes, integrals):
    lowered = amplitudes.astype(jnp.bfloat16)
    lowered = lax.optimization_barrier(lowered).astype(jnp.float32)
    left = lowered.reshape(I_SLAB * VIRTUAL, OCCUPIED * VIRTUAL)
    right = integrals.astype(jnp.float32).reshape(OCCUPIED * VIRTUAL, J_SLAB * VIRTUAL)
    cycle = jnp.dot(left, right, precision=lax.Precision.HIGHEST, preferred_element_type=jnp.float32)
    return cycle.reshape(I_SLAB, VIRTUAL, J_SLAB, VIRTUAL)
```

```python
import functools

import jax
import jax.numpy as jnp
from jax import lax
from jax.experimental import pallas as pl
from jax.experimental.pallas import tpu as pltpu
from jax.sharding import Mesh
from jax.sharding import PartitionSpec as P

LANES = 128
CHUNKS = (2, 2, 1, 1, 1, 1)


def gathered_body(amplitudes, integrals):
    slab_i, local_a, local_k, full_c = amplitudes.shape
    tiles = lax.axis_size("ta")
    tile_c = full_c // tiles
    lowered = amplitudes.astype(jnp.bfloat16)
    packed = lowered.reshape(slab_i, local_a, local_k, tiles, tile_c)
    packed = jnp.transpose(packed, (0, 1, 3, 2, 4)).reshape(
        slab_i, local_a, tiles, local_k * tile_c
    )
    moved = lax.all_to_all(
        lax.all_to_all(packed, "ta", split_axis=2, concat_axis=1, tiled=True),
        "row",
        split_axis=1,
        concat_axis=2,
        tiled=True,
    )
    rows_a = moved.shape[1]
    merged = moved.reshape(slab_i, rows_a, moved.shape[2] * moved.shape[3])
    count_j = integrals.shape[2]
    width_b = integrals.shape[3]
    cols_c = integrals.shape[1]
    gathered = lax.all_gather(integrals, "row", axis=0, tiled=True)
    left_side = merged.reshape(slab_i * rows_a, merged.shape[2])
    right_side = gathered.reshape(gathered.shape[0] * cols_c, count_j * width_b)
    partial_sum = jnp.dot(left_side, right_side, preferred_element_type=jnp.float32)
    partial_sum = partial_sum.reshape(slab_i, rows_a, count_j, width_b)
    return lax.psum_scatter(partial_sum, "ta", scatter_dimension=3, tiled=True)


def prep_kernel(la, lk, place, *refs):
    ins, outs = refs[:4], refs[4:]
    lane = lax.broadcasted_iota(jnp.int32, (la, LANES), 1)
    odd = (lane & 32) != 0
    up = place[1] * 64 + place[2] * 32
    down = lax.rem(place[1] * 64 + LANES - place[2] * 32, LANES)
    for src, dst in zip(ins, outs):
        for k in range(lk):
            rows = src[0, pl.ds(k, la, stride=lk), :]
            rows = jnp.where(odd, pltpu.roll(rows, up, 1), pltpu.roll(rows, down, 1))
            dst[0, k] = rows.astype(jnp.bfloat16)


def prep(amps, place, la, lk, start, count):
    out = jax.ShapeDtypeStruct((count, lk, la, LANES), jnp.bfloat16)
    return pl.pallas_call(
        functools.partial(prep_kernel, la, lk),
        out_shape=[out] * 4,
        grid_spec=pltpu.PrefetchScalarGridSpec(
            num_scalar_prefetch=1,
            grid=(count,),
            in_specs=[
                pl.BlockSpec((1, la * lk, LANES), lambda i, place, d=d: (start + i, 0, place[0] ^ d))
                for d in range(4)
            ],
            out_specs=[pl.BlockSpec((1, lk, la, LANES), lambda i, place: (i, 0, 0, 0))] * 4,
        ),
        compiler_params=pltpu.CompilerParams(vmem_limit_bytes=32 * 2**20),
        cost_estimate=pl.CostEstimate(
            flops=count * la * lk * 512, bytes_accessed=count * la * lk * 512 * 6, transcendentals=0
        ),
        name="prep",
    )(place, amps, amps, amps, amps)


def product_kernel(ni, kb, la, nj, place, *refs):
    ts, ws, out, acc = refs[:4], refs[4:8], refs[8], refs[9]
    step = pl.program_id(0)
    left = [
        jnp.concatenate([t[:, k].reshape(ni * la, LANES) for t in ts], axis=0) for k in range(kb)
    ]
    left = jnp.concatenate(left, axis=1)
    for j in range(nj):
        right = jnp.concatenate([w[k, j] for k in range(kb) for w in ws], axis=0)
        value = jnp.dot(left, right, preferred_element_type=jnp.float32)

        @pl.when(step == 0)
        def _():
            acc[j] = value

        @pl.when(step > 0)
        def _():
            acc[j] += value

    @pl.when(step == pl.num_programs(0) - 1)
    def _():
        high, low = place[0] >> 1, place[0] & 1
        for d in range(4):
            for q in range(4):
                for j in range(nj):
                    piece = acc[j, pl.ds(d * ni * la, ni * la), pl.ds(q * LANES, LANES)]
                    out[high ^ (d >> 1), q & 1, q >> 1, low ^ (d & 1), j] = piece.reshape(
                        ni, la, LANES
                    )


def product(place, ts, ws):
    ni, lk, la, _ = ts[0].shape
    nj, width = ws[0].shape[1], ws[0].shape[3]
    lc = ws[0].shape[2]
    kb = 8
    rows = 4 * ni * la
    out = jax.ShapeDtypeStruct((2, 2, 2, 2, nj, ni, la, LANES), jnp.float32)
    return pl.pallas_call(
        functools.partial(product_kernel, ni, kb, la, nj),
        out_shape=out,
        grid_spec=pltpu.PrefetchScalarGridSpec(
            num_scalar_prefetch=1,
            grid=(lk // kb,),
            in_specs=[pl.BlockSpec((ni, kb, la, LANES), lambda s, place: (0, s, 0, 0))] * 4
            + [pl.BlockSpec((kb, nj, lc, width), lambda s, place: (s, 0, 0, 0))] * 4,
            out_specs=pl.BlockSpec(out.shape, lambda s, place: (0,) * 8),
            scratch_shapes=[pltpu.VMEM((nj, rows, width), jnp.float32)],
        ),
        compiler_params=pltpu.CompilerParams(vmem_limit_bytes=48 * 2**20),
        cost_estimate=pl.CostEstimate(
            flops=2 * rows * nj * width * lk * 4 * lc,
            bytes_accessed=lk * 4 * lc * nj * width * 2 + rows * lk * LANES * 2 + rows * nj * width * 4,
            transcendentals=0,
        ),
        name="product",
    )(place, *ts, *ws)


def swapped(x, axis, bits=1):
    n = lax.axis_size(axis)
    return lax.ppermute(x, axis, [(s, s ^ bits) for s in range(n)])


def exchanged(x, axis, mine, bits=1):
    kept = lax.dynamic_index_in_dim(x, mine, 0, keepdims=False)
    sent = lax.dynamic_index_in_dim(x, 1 - mine, 0, keepdims=False)
    return kept + swapped(sent, axis, bits)


def tiled_body(amplitudes, integrals):
    ni, la, lk, full_c = amplitudes.shape
    z, x, core, row = (lax.axis_index(n) for n in ("z", "x", "core", "row"))
    place = jnp.stack([z, x, core]).astype(jnp.int32)
    amps = amplitudes.reshape(ni, la * lk, full_c)
    chunks = []
    start = 0
    parts = []
    for count in CHUNKS:
        parts.append(prep(amps, place, la, lk, start, count))
        start += count
    w_own = jnp.transpose(integrals, (0, 2, 1, 3))
    w_x = swapped(w_own, "x")
    w_core = swapped(w_own, "core")
    w_both = swapped(w_x, "core")
    ws = (w_own, w_core, w_x, w_both)
    token = None
    moved = []
    for own, *others in parts:
        moved.append((own, *(swapped(o, "z", d) for d, o in zip((1, 2, 3), others))))
    for ts in moved:
        total = product(place, ts, ws)
        total = exchanged(total, "row", row)
        total = exchanged(total, "z", z & 1, 1)
        total = exchanged(total, "z", z >> 1, 2)
        lows, nj, count, _, _ = total.shape
        total = total.reshape(lows, nj, count, la, 4, LANES // 4)
        total = jnp.transpose(total, (4, 2, 0, 3, 1, 5))
        total = lax.all_to_all(total, ("x", "core"), split_axis=0, concat_axis=0, tiled=True)
        total = jnp.transpose(total, (1, 2, 0, 3, 4, 5))
        chunks.append(total.reshape(count, lows * 4 * la, nj, LANES // 4))
    return jnp.concatenate(chunks, axis=0)


def solution(mesh):
    ta, rows = mesh.shape["ta"], mesh.shape["row"]

    def fn(amplitudes, integrals):
        ni, a, k, c = amplitudes.shape
        la, lk = a // ta, k // rows
        fits = ta == 16 and rows == 2 and c == 4 * LANES and la % 16 == 0 and lk % 8 == 0
        fits = fits and ni == sum(CHUNKS)
        if not fits:
            placed = (P(None, "ta", "row", None), P("row", "ta", None, None))
            return jax.shard_map(
                gathered_body,
                mesh=mesh,
                in_specs=placed,
                out_specs=P(None, "row", None, "ta"),
                check_vma=False,
            )(amplitudes, integrals)
        fine = Mesh(mesh.devices.reshape(4, 2, 2, 2), ("z", "x", "core", "row"))
        ta_axes = ("z", "x", "core")
        return jax.shard_map(
            tiled_body,
            mesh=fine,
            in_specs=(P(None, ta_axes, "row", None), P("row", ta_axes, None, None)),
            out_specs=P(None, "row", None, ta_axes),
            check_vma=False,
        )(amplitudes, integrals)

    return fn
```

```python
import functools

import jax
import jax.numpy as jnp
from jax import lax
from jax.experimental import pallas as pl
from jax.experimental.pallas import tpu as pltpu
from jax.sharding import Mesh
from jax.sharding import PartitionSpec as P

LANES = 128
CHUNKS = (1, 3, 2, 1, 1)
GROUPS = (4, 2, 1, 1)


def gathered_body(amplitudes, integrals):
    slab_i, local_a, local_k, full_c = amplitudes.shape
    tiles = lax.axis_size("ta")
    tile_c = full_c // tiles
    lowered = amplitudes.astype(jnp.bfloat16)
    packed = lowered.reshape(slab_i, local_a, local_k, tiles, tile_c)
    packed = jnp.transpose(packed, (0, 1, 3, 2, 4)).reshape(
        slab_i, local_a, tiles, local_k * tile_c
    )
    moved = lax.all_to_all(
        lax.all_to_all(packed, "ta", split_axis=2, concat_axis=1, tiled=True),
        "row",
        split_axis=1,
        concat_axis=2,
        tiled=True,
    )
    rows_a = moved.shape[1]
    merged = moved.reshape(slab_i, rows_a, moved.shape[2] * moved.shape[3])
    count_j = integrals.shape[2]
    width_b = integrals.shape[3]
    cols_c = integrals.shape[1]
    gathered = lax.all_gather(integrals, "row", axis=0, tiled=True)
    left_side = merged.reshape(slab_i * rows_a, merged.shape[2])
    right_side = gathered.reshape(gathered.shape[0] * cols_c, count_j * width_b)
    partial_sum = jnp.dot(left_side, right_side, preferred_element_type=jnp.float32)
    partial_sum = partial_sum.reshape(slab_i, rows_a, count_j, width_b)
    return lax.psum_scatter(partial_sum, "ta", scatter_dimension=3, tiled=True)


def prep_kernel(la, lk, n, place, *refs):
    ins, outs = refs[:n], refs[n:]
    lane = lax.broadcasted_iota(jnp.int32, (la, LANES), 1)
    odd = (lane & 32) != 0
    up = place[1] * 64 + place[2] * 32
    down = lax.rem(place[1] * 64 + LANES - place[2] * 32, LANES)
    for src, dst in zip(ins, outs):
        for k in range(lk):
            rows = src[0, pl.ds(k, la, stride=lk), :]
            rows = jnp.where(odd, pltpu.roll(rows, up, 1), pltpu.roll(rows, down, 1))
            dst[0, k] = rows.astype(jnp.bfloat16)


def prep(amps, place, la, lk, start, count, steps):
    n = len(steps)
    out = jax.ShapeDtypeStruct((count, lk, la, LANES), jnp.bfloat16)
    return pl.pallas_call(
        functools.partial(prep_kernel, la, lk, n),
        out_shape=[out] * n,
        grid_spec=pltpu.PrefetchScalarGridSpec(
            num_scalar_prefetch=1,
            grid=(count,),
            in_specs=[
                pl.BlockSpec((1, la * lk, LANES), lambda i, place, d=d: (start + i, 0, place[0] ^ d))
                for d in steps
            ],
            out_specs=[pl.BlockSpec((1, lk, la, LANES), lambda i, place: (i, 0, 0, 0))] * n,
        ),
        compiler_params=pltpu.CompilerParams(vmem_limit_bytes=60 * 2**20),
        cost_estimate=pl.CostEstimate(flops=int(5e9) * count * n, bytes_accessed=1000, transcendentals=0),
        name="prep",
    )(place, *([amps] * n))


def product_kernel(ni, kb, la, nj, place, *refs):
    ts, ws, out, acc = refs[: 4 * ni], refs[4 * ni : 4 * ni + 4], refs[-2], refs[-1]
    step = pl.program_id(0)
    left = [
        jnp.concatenate([t[0, k] for t in ts], axis=0) for k in range(kb)
    ]
    left = jnp.concatenate(left, axis=1)
    for j in range(nj):
        right = jnp.concatenate([w[k, j] for k in range(kb) for w in ws], axis=0)
        value = jnp.dot(left, right, preferred_element_type=jnp.float32)

        @pl.when(step == 0)
        def _():
            acc[j] = value

        @pl.when(step > 0)
        def _():
            acc[j] += value

    @pl.when(step == pl.num_programs(0) - 1)
    def _():
        high, low = place[0] >> 1, place[0] & 1
        for d in range(4):
            for q in range(4):
                for j in range(nj):
                    piece = acc[j, pl.ds(d * ni * la, ni * la), pl.ds(q * LANES, LANES)]
                    out[high ^ (d >> 1), q & 1, q >> 1, low ^ (d & 1), j] = piece.reshape(
                        ni, la, LANES
                    )


def product(place, sources, ws):
    ni = len(sources[0])
    _, lk, la, _ = sources[0][0][0].shape
    nj, width = ws[0].shape[1], ws[0].shape[3]
    lc = ws[0].shape[2]
    kb = 8
    rows = 4 * ni * la
    flat = [pair for source in sources for pair in source]
    out = jax.ShapeDtypeStruct((2, 2, 2, 2, nj, ni, la, LANES), jnp.float32)
    return pl.pallas_call(
        functools.partial(product_kernel, ni, kb, la, nj),
        out_shape=out,
        grid_spec=pltpu.PrefetchScalarGridSpec(
            num_scalar_prefetch=1,
            grid=(lk // kb,),
            in_specs=[
                pl.BlockSpec((1, kb, la, LANES), lambda s, place, at=at: (at, s, 0, 0))
                for _, at in flat
            ]
            + [pl.BlockSpec((kb, nj, lc, width), lambda s, place: (s, 0, 0, 0))] * 4,
            out_specs=pl.BlockSpec(out.shape, lambda s, place: (0,) * 8),
            scratch_shapes=[pltpu.VMEM((nj, rows, width), jnp.float32)],
        ),
        compiler_params=pltpu.CompilerParams(vmem_limit_bytes=60 * 2**20),
        cost_estimate=pl.CostEstimate(flops=2 * rows * nj * width * lk * 4 * lc * 2, bytes_accessed=1000, transcendentals=0),
        name="product",
    )(place, *[array for array, _ in flat], *ws)


def gated(arrays, *after):
    arrays = tuple(arrays)
    return pl.pallas_call(
        lambda *refs: None,
        out_shape=[jax.ShapeDtypeStruct(a.shape, a.dtype) for a in arrays],
        in_specs=[pl.BlockSpec(memory_space=pl.ANY)] * (len(arrays) + len(after)),
        out_specs=[pl.BlockSpec(memory_space=pl.ANY)] * len(arrays),
        input_output_aliases={n: n for n in range(len(arrays))},
        compiler_params=pltpu.CompilerParams(vmem_limit_bytes=60 * 2**20),
        cost_estimate=pl.CostEstimate(flops=1000, bytes_accessed=1000, transcendentals=0),
        name="gate",
    )(*arrays, *after)


def swapped(x, axis, bits=1):
    n = lax.axis_size(axis)
    return lax.ppermute(x, axis, [(s, s ^ bits) for s in range(n)])


def exchanged(x, axis, mine, bits=1):
    kept = lax.dynamic_index_in_dim(x, mine, 0, keepdims=False)
    sent = lax.dynamic_index_in_dim(x, 1 - mine, 0, keepdims=False)
    return kept + swapped(sent, axis, bits)


def finish_kernel(nj, place, *refs):
    pieces, out, turned = refs[:4], refs[-2], refs[-1]
    inner = 2 * place[1] + place[2]
    lane = lax.broadcasted_iota(jnp.int32, (32, LANES), 1)
    odd = (lane & 32) != 0
    up = place[1] * 64 + place[2] * 32
    down = lax.rem(place[1] * 64 + LANES - place[2] * 32, LANES)
    for low in range(2):
        for j in range(nj):
            rows = jnp.concatenate([piece[low, j, 0] for piece in pieces], axis=0)
            turned[...] = rows.T
            own = turned[pl.ds(pl.multiple_of(32 * inner, 32), 32), :]
            own = jnp.where(odd, pltpu.roll(own, up, 1), pltpu.roll(own, down, 1))
            out[0, j, :, low * LANES : (low + 1) * LANES] = own


def finish(place, pieces, start, slab_i, before):
    lows, nj, count, la, _ = pieces[0].shape
    out = jax.ShapeDtypeStruct((slab_i, nj, 32, lows * 4 * la), jnp.float32)
    args, specs, alias = [], [], {}
    if before is not None:
        args, specs, alias = [before], [pl.BlockSpec(memory_space=pl.ANY)], {5: 0}
    return pl.pallas_call(
        functools.partial(finish_kernel, nj),
        out_shape=out,
        grid_spec=pltpu.PrefetchScalarGridSpec(
            num_scalar_prefetch=1,
            grid=(count,),
            in_specs=[
                pl.BlockSpec((lows, nj, 1, la, LANES), lambda i, place: (0, 0, i, 0, 0))
            ]
            * 4
            + specs,
            out_specs=pl.BlockSpec((1, nj, 32, lows * 4 * la), lambda i, place: (start + i, 0, 0, 0)),
            scratch_shapes=[pltpu.VMEM((LANES, LANES), jnp.float32)],
        ),
        input_output_aliases=alias,
        compiler_params=pltpu.CompilerParams(vmem_limit_bytes=60 * 2**20),
        cost_estimate=pl.CostEstimate(flops=1000, bytes_accessed=1000, transcendentals=0),
        name="finish",
    )(place, *pieces, *args)


def tiled_body(amplitudes, integrals):
    ni, la, lk, full_c = amplitudes.shape
    z, x, core, row = (lax.axis_index(n) for n in ("z", "x", "core", "row"))
    place = jnp.stack([z, x, core]).astype(jnp.int32)
    amps = amplitudes.reshape(ni, la * lk, full_c)
    counts = CHUNKS
    starts = [sum(counts[:n]) for n in range(len(counts))]
    parts = [prep(amps, place, la, lk, s, c, (2, 3)) for s, c in zip(starts, counts)]
    integrals, *parts[0] = lax.optimization_barrier((integrals, *parts[0]))
    moved = [(swapped(two, "z", 2), swapped(three, "z", 3)) for two, three in parts]
    w_own = jnp.transpose(integrals, (0, 2, 1, 3))
    w_x = swapped(w_own, "x")
    w_core = swapped(w_own, "core")
    (later,) = gated((place,), parts[0][0], parts[1][0], w_own)
    own, one = prep(amps, later, la, lk, 0, ni, (0, 1))
    one = swapped(one, "z", 1)
    (w_x,) = gated((w_x,), *moved[0], *moved[1], one, *[p[0] for p in parts[2:]])
    w_both = swapped(w_x, "core")
    ws = (w_own, w_core, w_x, w_both)

    where = [(m, i) for m, count in enumerate(counts) for i in range(count)]
    totals = []
    n = 0
    for g, count in enumerate(GROUPS):
        at = range(n, n + count)
        n += count
        two = [(moved[where[i][0]][0], where[i][1]) for i in at]
        three = [(moved[where[i][0]][1], where[i][1]) for i in at]
        totals.append(product(place, ([(own, i) for i in at], [(one, i) for i in at], two, three), ws))

    def exchange(total, axis, mine, bits, *after):
        kept = lax.dynamic_index_in_dim(total, mine, 0, keepdims=False)
        sent = lax.dynamic_index_in_dim(total, 1 - mine, 0, keepdims=False)
        if after:
            (sent,) = gated((sent,), *after)
        return kept + swapped(sent, axis, bits)

    result = None
    rows, lows, highs = [], [], []
    for g, total in enumerate(totals):
        rows.append(exchange(total, "row", row, 1, *rows[g - 1 : g], *lows[max(g - 2, 0) : max(g - 1, 0)]))
        lows.append(exchange(rows[g], "z", z & 1, 1, *lows[max(g - 1, 0) : g]))
        highs.append(exchange(lows[g], "z", z >> 1, 2))
    for g, total in enumerate(highs):
        pieces = [total]
        for bits in (1, 2, 3):
            pairs = [(s, s ^ bits) for s in range(4)]
            pieces.append(lax.ppermute(total, ("x", "core"), pairs))
        result = finish(place, pieces, sum(GROUPS[:g]), ni, result)
    return jnp.transpose(result, (0, 3, 1, 2))


def solution(mesh):
    ta, rows = mesh.shape["ta"], mesh.shape["row"]

    def fn(amplitudes, integrals):
        ni, a, k, c = amplitudes.shape
        la, lk = a // ta, k // rows
        fits = ta == 16 and rows == 2 and c == 4 * LANES and la % 16 == 0 and lk % 8 == 0
        fits = fits and ni == sum(GROUPS)
        if not fits:
            placed = (P(None, "ta", "row", None), P("row", "ta", None, None))
            return jax.shard_map(
                gathered_body,
                mesh=mesh,
                in_specs=placed,
                out_specs=P(None, "row", None, "ta"),
                check_vma=False,
            )(amplitudes, integrals)
        fine = Mesh(mesh.devices.reshape(4, 2, 2, 2), ("z", "x", "core", "row"))
        ta_axes = ("z", "x", "core")
        return jax.shard_map(
            tiled_body,
            mesh=fine,
            in_specs=(P(None, ta_axes, "row", None), P("row", ta_axes, None, None)),
            out_specs=P(None, "row", None, ta_axes),
            check_vma=False,
        )(amplitudes, integrals)

    return fn
```

```python
import functools

import jax
import jax.numpy as jnp
from jax import lax
from jax.experimental import pallas as pl
from jax.experimental.pallas import tpu as pltpu
from jax.sharding import Mesh
from jax.sharding import PartitionSpec as P

LANES = 128
CHUNKS = (1, 3, 2, 1, 1)
GROUPS = (4, 2, 1, 1)
CHAINED = 2


def gathered_body(amplitudes, integrals):
    slab_i, local_a, local_k, full_c = amplitudes.shape
    tiles = lax.axis_size("ta")
    tile_c = full_c // tiles
    lowered = amplitudes.astype(jnp.bfloat16)
    packed = lowered.reshape(slab_i, local_a, local_k, tiles, tile_c)
    packed = jnp.transpose(packed, (0, 1, 3, 2, 4)).reshape(
        slab_i, local_a, tiles, local_k * tile_c
    )
    moved = lax.all_to_all(
        lax.all_to_all(packed, "ta", split_axis=2, concat_axis=1, tiled=True),
        "row",
        split_axis=1,
        concat_axis=2,
        tiled=True,
    )
    rows_a = moved.shape[1]
    merged = moved.reshape(slab_i, rows_a, moved.shape[2] * moved.shape[3])
    count_j = integrals.shape[2]
    width_b = integrals.shape[3]
    cols_c = integrals.shape[1]
    gathered = lax.all_gather(integrals, "row", axis=0, tiled=True)
    left_side = merged.reshape(slab_i * rows_a, merged.shape[2])
    right_side = gathered.reshape(gathered.shape[0] * cols_c, count_j * width_b)
    partial_sum = jnp.dot(left_side, right_side, preferred_element_type=jnp.float32)
    partial_sum = partial_sum.reshape(slab_i, rows_a, count_j, width_b)
    return lax.psum_scatter(partial_sum, "ta", scatter_dimension=3, tiled=True)


def prep_kernel(la, lk, n, place, *refs):
    ins, outs = refs[:n], refs[n:]
    lane = lax.broadcasted_iota(jnp.int32, (la, LANES), 1)
    odd = (lane & 32) != 0
    up = place[1] * 64 + place[2] * 32
    down = lax.rem(place[1] * 64 + LANES - place[2] * 32, LANES)
    for src, dst in zip(ins, outs):
        for k in range(lk):
            rows = src[0, pl.ds(k, la, stride=lk), :]
            rows = jnp.where(odd, pltpu.roll(rows, up, 1), pltpu.roll(rows, down, 1))
            dst[0, k] = rows.astype(jnp.bfloat16)


def prep(amps, place, la, lk, start, count, steps):
    n = len(steps)
    out = jax.ShapeDtypeStruct((count, lk, la, LANES), jnp.bfloat16)
    return pl.pallas_call(
        functools.partial(prep_kernel, la, lk, n),
        out_shape=[out] * n,
        grid_spec=pltpu.PrefetchScalarGridSpec(
            num_scalar_prefetch=1,
            grid=(count,),
            in_specs=[
                pl.BlockSpec((1, la * lk, LANES), lambda i, place, d=d: (start + i, 0, place[0] ^ d))
                for d in steps
            ],
            out_specs=[pl.BlockSpec((1, lk, la, LANES), lambda i, place: (i, 0, 0, 0))] * n,
        ),
        compiler_params=pltpu.CompilerParams(vmem_limit_bytes=60 * 2**20),
        cost_estimate=pl.CostEstimate(flops=int(5e9) * count * n, bytes_accessed=1000, transcendentals=0),
        name="prep",
    )(place, *([amps] * n))


def store_halves(ni, la, nj, place, out, acc):
    high, low = place[0] >> 1, place[0] & 1
    for d in range(4):
        for q in range(4):
            for j in range(nj):
                piece = acc[j, pl.ds(d * ni * la, ni * la), pl.ds(q * LANES, LANES)]
                out[high ^ (d >> 1), q & 1, q >> 1, low ^ (d & 1), j] = piece.reshape(ni, la, LANES)


def store_turned(ni, la, nj, place, out, acc):
    high, low = place[0] >> 1, place[0] & 1
    for half in range(2):
        for q in range(4):
            for pair in range(nj // 2):
                blocks = []
                for j in (2 * pair, 2 * pair + 1):
                    for side in range(2):
                        at = pl.multiple_of((2 * half + (low ^ side)) * la, la)
                        blocks.append(acc[j, pl.ds(at, la), pl.ds(q * LANES, LANES)])
                turned = jnp.concatenate(blocks, axis=0).T.astype(jnp.bfloat16)
                for n in range(4):
                    out[q, n, high ^ half, pair] = turned[32 * n : 32 * (n + 1), :]


def product_kernel(store, ni, kb, la, nj, place, *refs):
    ts, ws, out, acc = refs[: 4 * ni], refs[4 * ni : 4 * ni + 4], refs[-2], refs[-1]
    step = pl.program_id(0)
    left = [
        jnp.concatenate([t[0, k] for t in ts], axis=0) for k in range(kb)
    ]
    left = jnp.concatenate(left, axis=1)
    for j in range(nj):
        right = jnp.concatenate([w[k, j] for k in range(kb) for w in ws], axis=0)
        value = jnp.dot(left, right, preferred_element_type=jnp.float32)

        @pl.when(step == 0)
        def _():
            acc[j] = value

        @pl.when(step > 0)
        def _():
            acc[j] += value

    @pl.when(step == pl.num_programs(0) - 1)
    def _():
        store(ni, la, nj, place, out, acc)


def product(place, sources, ws, last):
    ni = len(sources[0])
    _, lk, la, _ = sources[0][0][0].shape
    nj, width = ws[0].shape[1], ws[0].shape[3]
    lc = ws[0].shape[2]
    kb = 8
    rows = 4 * ni * la
    flat = [pair for source in sources for pair in source]
    shape = (4, 4, 2, nj // 2, 32, LANES) if last else (2, 2, 2, 2, nj, ni, la, LANES)
    store = store_turned if last else store_halves
    out = jax.ShapeDtypeStruct(shape, jnp.bfloat16 if last else jnp.float32)
    return pl.pallas_call(
        functools.partial(product_kernel, store, ni, kb, la, nj),
        out_shape=out,
        grid_spec=pltpu.PrefetchScalarGridSpec(
            num_scalar_prefetch=1,
            grid=(lk // kb,),
            in_specs=[
                pl.BlockSpec((1, kb, la, LANES), lambda s, place, at=at: (at, s, 0, 0))
                for _, at in flat
            ]
            + [pl.BlockSpec((kb, nj, lc, width), lambda s, place: (s, 0, 0, 0))] * 4,
            out_specs=pl.BlockSpec(shape, lambda s, place: (0,) * len(shape)),
            scratch_shapes=[pltpu.VMEM((nj, rows, width), jnp.float32)],
        ),
        compiler_params=pltpu.CompilerParams(vmem_limit_bytes=60 * 2**20),
        cost_estimate=pl.CostEstimate(flops=2 * rows * nj * width * lk * 4 * lc * 3, bytes_accessed=1000, transcendentals=0),
        name="product",
    )(place, *[array for array, _ in flat], *ws)


def gated(arrays, *after):
    arrays = tuple(arrays)
    return pl.pallas_call(
        lambda *refs: None,
        out_shape=[jax.ShapeDtypeStruct(a.shape, a.dtype) for a in arrays],
        in_specs=[pl.BlockSpec(memory_space=pl.ANY)] * (len(arrays) + len(after)),
        out_specs=[pl.BlockSpec(memory_space=pl.ANY)] * len(arrays),
        input_output_aliases={n: n for n in range(len(arrays))},
        compiler_params=pltpu.CompilerParams(vmem_limit_bytes=60 * 2**20),
        cost_estimate=pl.CostEstimate(flops=1000, bytes_accessed=1000, transcendentals=0),
        name="gate",
    )(*arrays, *after)


def swapped(x, axis, bits=1):
    n = lax.axis_size(axis)
    return lax.ppermute(x, axis, [(s, s ^ bits) for s in range(n)])


def finish_kernel(nj, place, *refs):
    pieces, out, turned = refs[:4], refs[-2], refs[-1]
    inner = 2 * place[1] + place[2]
    lane = lax.broadcasted_iota(jnp.int32, (32, LANES), 1)
    odd = (lane & 32) != 0
    up = place[1] * 64 + place[2] * 32
    down = lax.rem(place[1] * 64 + LANES - place[2] * 32, LANES)
    for low in range(2):
        for j in range(nj):
            rows = jnp.concatenate([piece[low, j, 0] for piece in pieces], axis=0)
            turned[...] = rows.T
            own = turned[pl.ds(pl.multiple_of(32 * inner, 32), 32), :]
            own = jnp.where(odd, pltpu.roll(own, up, 1), pltpu.roll(own, down, 1))
            out[0, j, :, low * LANES : (low + 1) * LANES] = own


def finish(place, pieces, start, slab_i, before):
    lows, nj, count, la, _ = pieces[0].shape
    out = jax.ShapeDtypeStruct((slab_i, nj, 32, lows * 4 * la), jnp.float32)
    args, specs, alias = [], [], {}
    if before is not None:
        args, specs, alias = [before], [pl.BlockSpec(memory_space=pl.ANY)], {5: 0}
    return pl.pallas_call(
        functools.partial(finish_kernel, nj),
        out_shape=out,
        grid_spec=pltpu.PrefetchScalarGridSpec(
            num_scalar_prefetch=1,
            grid=(count,),
            in_specs=[
                pl.BlockSpec((lows, nj, 1, la, LANES), lambda i, place: (0, 0, i, 0, 0))
            ]
            * 4
            + specs,
            out_specs=pl.BlockSpec((1, nj, 32, lows * 4 * la), lambda i, place: (start + i, 0, 0, 0)),
            scratch_shapes=[pltpu.VMEM((LANES, LANES), jnp.float32)],
        ),
        input_output_aliases=alias,
        compiler_params=pltpu.CompilerParams(vmem_limit_bytes=60 * 2**20),
        cost_estimate=pl.CostEstimate(flops=1000, bytes_accessed=1000, transcendentals=0),
        name="finish",
    )(place, *pieces, *args)


def gather_kernel(nj, came, before, out):
    block = lax.broadcasted_iota(jnp.int32, (32, LANES), 1) >> 5
    for pair in range(nj // 2):
        sums = []
        for n in range(4):
            total = came[0, n, 0, pair].astype(jnp.float32)
            for zs in range(4):
                for r in range(2):
                    if zs + r > 0:
                        total += came[zs, n, r, pair].astype(jnp.float32)
            sums.append(total)
        for m in range(4):
            value = None
            for n in range(4):
                turned = sums[n] if n == m else pltpu.roll(sums[n], (32 * (n - m)) % LANES, 1)
                value = turned if n == 0 else jnp.where(block == n, turned, value)
            low = m & 1
            out[0, 2 * pair + (m >> 1), :, low * LANES : (low + 1) * LANES] = value


def gather(came, before, at):
    _, nj, wide, width = before.shape
    return pl.pallas_call(
        functools.partial(gather_kernel, nj),
        out_shape=jax.ShapeDtypeStruct(before.shape, before.dtype),
        grid=(1,),
        in_specs=[
            pl.BlockSpec(came.shape, lambda i: (0,) * 6),
            pl.BlockSpec(memory_space=pl.ANY),
        ],
        out_specs=pl.BlockSpec((1, nj, wide, width), lambda i: (at, 0, 0, 0)),
        input_output_aliases={1: 0},
        compiler_params=pltpu.CompilerParams(vmem_limit_bytes=60 * 2**20),
        cost_estimate=pl.CostEstimate(flops=1000, bytes_accessed=1000, transcendentals=0),
        name="gather",
    )(came, before)


def tiled_body(amplitudes, integrals):
    ni, la, lk, full_c = amplitudes.shape
    z, x, core, row = (lax.axis_index(n) for n in ("z", "x", "core", "row"))
    place = jnp.stack([z, x, core]).astype(jnp.int32)
    amps = amplitudes.reshape(ni, la * lk, full_c)
    counts = CHUNKS
    starts = [sum(counts[:n]) for n in range(len(counts))]
    parts = [prep(amps, place, la, lk, s, c, (2, 3)) for s, c in zip(starts, counts)]
    integrals, *parts[0] = lax.optimization_barrier((integrals, *parts[0]))
    moved = [(swapped(two, "z", 2), swapped(three, "z", 3)) for two, three in parts]
    w_own = jnp.transpose(integrals, (0, 2, 1, 3))
    w_x = swapped(w_own, "x")
    w_core = swapped(w_own, "core")
    (later,) = gated((place,), parts[0][0], parts[1][0], w_own)
    own, one = prep(amps, later, la, lk, 0, ni, (0, 1))
    one = swapped(one, "z", 1)
    (w_x,) = gated((w_x,), *moved[0], *moved[1], one, *[p[0] for p in parts[2:]])
    w_both = swapped(w_x, "core")
    ws = (w_own, w_core, w_x, w_both)

    where = [(m, i) for m, count in enumerate(counts) for i in range(count)]
    totals = []
    n = 0
    for g, count in enumerate(GROUPS):
        at = range(n, n + count)
        n += count
        two = [(moved[where[i][0]][0], where[i][1]) for i in at]
        three = [(moved[where[i][0]][1], where[i][1]) for i in at]
        totals.append(product(place, ([(own, i) for i in at], [(one, i) for i in at], two, three), ws, g >= CHAINED))

    def exchange(total, axis, mine, bits, *after):
        kept = lax.dynamic_index_in_dim(total, mine, 0, keepdims=False)
        sent = lax.dynamic_index_in_dim(total, 1 - mine, 0, keepdims=False)
        if after:
            (sent,) = gated((sent,), *after)
        if bits == 2:
            return kept + swapped(sent.astype(jnp.bfloat16), axis, bits).astype(jnp.float32)
        return kept + swapped(sent, axis, bits)

    result = None
    rows, lows, highs = [], [], []
    for g, total in enumerate(totals[:CHAINED]):
        rows.append(exchange(total, "row", row, 1, *rows[g - 1 : g], *lows[max(g - 2, 0) : max(g - 1, 0)]))
        lows.append(exchange(rows[g], "z", z & 1, 1, *lows[max(g - 1, 0) : g]))
        highs.append(exchange(lows[g], "z", z >> 1, 2))
    for g, total in enumerate(highs):
        pieces = [total]
        for bits in (1, 2, 3):
            pairs = [(s, s ^ bits) for s in range(4)]
            pieces.append(lax.ppermute(total, ("x", "core"), pairs))
        result = finish(place, pieces, sum(GROUPS[:g]), ni, result)
    for g, total in enumerate(totals[CHAINED:], CHAINED):
        came = total.reshape(32, -1, 32, LANES)
        came = lax.all_to_all(came, ("z", "x", "core", "row"), split_axis=0, concat_axis=0, tiled=True)
        result = gather(came.reshape(total.shape), result, sum(GROUPS[:g]))
    return jnp.transpose(result, (0, 3, 1, 2))


def solution(mesh):
    ta, rows = mesh.shape["ta"], mesh.shape["row"]

    def fn(amplitudes, integrals):
        ni, a, k, c = amplitudes.shape
        la, lk = a // ta, k // rows
        fits = ta == 16 and rows == 2 and c == 4 * LANES and la % 16 == 0 and lk % 8 == 0
        fits = fits and ni == sum(GROUPS)
        if not fits:
            placed = (P(None, "ta", "row", None), P("row", "ta", None, None))
            return jax.shard_map(
                gathered_body,
                mesh=mesh,
                in_specs=placed,
                out_specs=P(None, "row", None, "ta"),
                check_vma=False,
            )(amplitudes, integrals)
        fine = Mesh(mesh.devices.reshape(4, 2, 2, 2), ("z", "x", "core", "row"))
        ta_axes = ("z", "x", "core")
        return jax.shard_map(
            tiled_body,
            mesh=fine,
            in_specs=(P(None, ta_axes, "row", None), P("row", ta_axes, None, None)),
            out_specs=P(None, "row", None, ta_axes),
            check_vma=False,
        )(amplitudes, integrals)

    return fn
```

```python
import functools

import jax
import jax.numpy as jnp
from jax import lax
from jax.experimental import pallas as pl
from jax.experimental.pallas import tpu as pltpu
from jax.sharding import Mesh
from jax.sharding import PartitionSpec as P

LANES = 128
CHUNKS = (1, 3, 2, 1, 1)
GROUPS = (4, 2, 1, 1)
CHAINED = 2


def gathered_body(amplitudes, integrals):
    slab_i, local_a, local_k, full_c = amplitudes.shape
    tiles = lax.axis_size("ta")
    tile_c = full_c // tiles
    lowered = amplitudes.astype(jnp.bfloat16)
    packed = lowered.reshape(slab_i, local_a, local_k, tiles, tile_c)
    packed = jnp.transpose(packed, (0, 1, 3, 2, 4)).reshape(
        slab_i, local_a, tiles, local_k * tile_c
    )
    moved = lax.all_to_all(
        lax.all_to_all(packed, "ta", split_axis=2, concat_axis=1, tiled=True),
        "row",
        split_axis=1,
        concat_axis=2,
        tiled=True,
    )
    rows_a = moved.shape[1]
    merged = moved.reshape(slab_i, rows_a, moved.shape[2] * moved.shape[3])
    count_j = integrals.shape[2]
    width_b = integrals.shape[3]
    cols_c = integrals.shape[1]
    gathered = lax.all_gather(integrals, "row", axis=0, tiled=True)
    left_side = merged.reshape(slab_i * rows_a, merged.shape[2])
    right_side = gathered.reshape(gathered.shape[0] * cols_c, count_j * width_b)
    partial_sum = jnp.dot(left_side, right_side, preferred_element_type=jnp.float32)
    partial_sum = partial_sum.reshape(slab_i, rows_a, count_j, width_b)
    return lax.psum_scatter(partial_sum, "ta", scatter_dimension=3, tiled=True)


def prep_kernel(la, lk, n, place, *refs):
    ins, outs = refs[:n], refs[n:]
    lane = lax.broadcasted_iota(jnp.int32, (la, LANES), 1)
    odd = (lane & 32) != 0
    up = place[1] * 64 + place[2] * 32
    down = lax.rem(place[1] * 64 + LANES - place[2] * 32, LANES)
    for src, dst in zip(ins, outs):
        for k in range(lk):
            rows = src[0, pl.ds(k, la, stride=lk), :]
            rows = jnp.where(odd, pltpu.roll(rows, up, 1), pltpu.roll(rows, down, 1))
            dst[0, k] = rows.astype(jnp.bfloat16)


def prep(amps, place, la, lk, start, count, steps):
    n = len(steps)
    out = jax.ShapeDtypeStruct((count, lk, la, LANES), jnp.bfloat16)
    return pl.pallas_call(
        functools.partial(prep_kernel, la, lk, n),
        out_shape=[out] * n,
        grid_spec=pltpu.PrefetchScalarGridSpec(
            num_scalar_prefetch=1,
            grid=(count,),
            in_specs=[
                pl.BlockSpec((1, la * lk, LANES), lambda i, place, d=d: (start + i, 0, place[0] ^ d))
                for d in steps
            ],
            out_specs=[pl.BlockSpec((1, lk, la, LANES), lambda i, place: (i, 0, 0, 0))] * n,
        ),
        compiler_params=pltpu.CompilerParams(vmem_limit_bytes=60 * 2**20),
        cost_estimate=pl.CostEstimate(flops=int(5e9) * count * n, bytes_accessed=1000, transcendentals=0),
        name="prep",
    )(place, *([amps] * n))


def store_halves(ni, la, nj, place, out, acc):
    high, low = place[0] >> 1, place[0] & 1
    for d in range(4):
        for q in range(4):
            for j in range(nj):
                piece = acc[j, pl.ds(d * ni * la, ni * la), pl.ds(q * LANES, LANES)]
                out[high ^ (d >> 1), q & 1, q >> 1, low ^ (d & 1), j] = piece.reshape(ni, la, LANES)


def store_turned(ni, la, nj, place, out, acc):
    high, low = place[0] >> 1, place[0] & 1
    for half in range(2):
        for q in range(4):
            for pair in range(nj // 2):
                blocks = []
                for j in (2 * pair, 2 * pair + 1):
                    for side in range(2):
                        at = pl.multiple_of((2 * half + (low ^ side)) * la, la)
                        blocks.append(acc[j, pl.ds(at, la), pl.ds(q * LANES, LANES)])
                turned = jnp.concatenate(blocks, axis=0).T.astype(jnp.bfloat16)
                for n in range(4):
                    out[q, n, high ^ half, pair] = turned[32 * n : 32 * (n + 1), :]


def product_kernel(store, ni, kb, la, nj, place, *refs):
    ts, ws, out, acc = refs[: 4 * ni], refs[4 * ni : 4 * ni + 4], refs[-2], refs[-1]
    step = pl.program_id(0)
    left = [
        jnp.concatenate([t[0, k] for t in ts], axis=0) for k in range(kb)
    ]
    left = jnp.concatenate(left, axis=1)
    for j in range(nj):
        right = jnp.concatenate([w[k, j] for k in range(kb) for w in ws], axis=0)
        value = jnp.dot(left, right, preferred_element_type=jnp.float32)

        @pl.when(step == 0)
        def _():
            acc[j] = value

        @pl.when(step > 0)
        def _():
            acc[j] += value

    @pl.when(step == pl.num_programs(0) - 1)
    def _():
        store(ni, la, nj, place, out, acc)


def product(place, sources, ws, last):
    ni = len(sources[0])
    _, lk, la, _ = sources[0][0][0].shape
    nj, width = ws[0].shape[1], ws[0].shape[3]
    lc = ws[0].shape[2]
    kb = 8
    rows = 4 * ni * la
    flat = [pair for source in sources for pair in source]
    shape = (4, 4, 2, nj // 2, 32, LANES) if last else (2, 2, 2, 2, nj, ni, la, LANES)
    store = store_turned if last else store_halves
    out = jax.ShapeDtypeStruct(shape, jnp.bfloat16 if last else jnp.float32)
    return pl.pallas_call(
        functools.partial(product_kernel, store, ni, kb, la, nj),
        out_shape=out,
        grid_spec=pltpu.PrefetchScalarGridSpec(
            num_scalar_prefetch=1,
            grid=(lk // kb,),
            in_specs=[
                pl.BlockSpec((1, kb, la, LANES), lambda s, place, at=at: (at, s, 0, 0))
                for _, at in flat
            ]
            + [pl.BlockSpec((kb, nj, lc, width), lambda s, place: (s, 0, 0, 0))] * 4,
            out_specs=pl.BlockSpec(shape, lambda s, place: (0,) * len(shape)),
            scratch_shapes=[pltpu.VMEM((nj, rows, width), jnp.float32)],
        ),
        compiler_params=pltpu.CompilerParams(vmem_limit_bytes=60 * 2**20),
        cost_estimate=pl.CostEstimate(flops=2 * rows * nj * width * lk * 4 * lc * 3, bytes_accessed=1000, transcendentals=0),
        name="product",
    )(place, *[array for array, _ in flat], *ws)


def gated(arrays, *after):
    arrays = tuple(arrays)
    return pl.pallas_call(
        lambda *refs: None,
        out_shape=[jax.ShapeDtypeStruct(a.shape, a.dtype) for a in arrays],
        in_specs=[pl.BlockSpec(memory_space=pl.ANY)] * (len(arrays) + len(after)),
        out_specs=[pl.BlockSpec(memory_space=pl.ANY)] * len(arrays),
        input_output_aliases={n: n for n in range(len(arrays))},
        compiler_params=pltpu.CompilerParams(vmem_limit_bytes=60 * 2**20),
        cost_estimate=pl.CostEstimate(flops=1000, bytes_accessed=1000, transcendentals=0),
        name="gate",
    )(*arrays, *after)


def swapped(x, axis, bits=1):
    n = lax.axis_size(axis)
    return lax.ppermute(x, axis, [(s, s ^ bits) for s in range(n)])


def finish_kernel(nj, place, *refs):
    pieces, out, turned = refs[:4], refs[-2], refs[-1]
    inner = 2 * place[1] + place[2]
    lane = lax.broadcasted_iota(jnp.int32, (32, LANES), 1)
    odd = (lane & 32) != 0
    up = place[1] * 64 + place[2] * 32
    down = lax.rem(place[1] * 64 + LANES - place[2] * 32, LANES)
    for low in range(2):
        for j in range(nj):
            rows = jnp.concatenate([piece[low, j, 0] for piece in pieces], axis=0)
            turned[...] = rows.T
            own = turned[pl.ds(pl.multiple_of(32 * inner, 32), 32), :]
            own = jnp.where(odd, pltpu.roll(own, up, 1), pltpu.roll(own, down, 1))
            out[0, j, :, low * LANES : (low + 1) * LANES] = own


def finish(place, pieces, start, slab_i, before):
    lows, nj, count, la, _ = pieces[0].shape
    out = jax.ShapeDtypeStruct((slab_i, nj, 32, lows * 4 * la), jnp.float32)
    args, specs, alias = [], [], {}
    if before is not None:
        args, specs, alias = [before], [pl.BlockSpec(memory_space=pl.ANY)], {5: 0}
    return pl.pallas_call(
        functools.partial(finish_kernel, nj),
        out_shape=out,
        grid_spec=pltpu.PrefetchScalarGridSpec(
            num_scalar_prefetch=1,
            grid=(count,),
            in_specs=[
                pl.BlockSpec((lows, nj, 1, la, LANES), lambda i, place: (0, 0, i, 0, 0))
            ]
            * 4
            + specs,
            out_specs=pl.BlockSpec((1, nj, 32, lows * 4 * la), lambda i, place: (start + i, 0, 0, 0)),
            scratch_shapes=[pltpu.VMEM((LANES, LANES), jnp.float32)],
        ),
        input_output_aliases=alias,
        compiler_params=pltpu.CompilerParams(vmem_limit_bytes=60 * 2**20),
        cost_estimate=pl.CostEstimate(flops=1000, bytes_accessed=1000, transcendentals=0),
        name="finish",
    )(place, *pieces, *args)


def gather_kernel(nj, came, before, out):
    block = lax.broadcasted_iota(jnp.int32, (32, LANES), 1) >> 5
    for pair in range(nj // 2):
        sums = []
        for n in range(4):
            total = came[0, n, 0, pair].astype(jnp.float32)
            for zs in range(4):
                for r in range(2):
                    if zs + r > 0:
                        total += came[zs, n, r, pair].astype(jnp.float32)
            sums.append(total)
        for m in range(4):
            value = None
            for n in range(4):
                turned = sums[n] if n == m else pltpu.roll(sums[n], (32 * (n - m)) % LANES, 1)
                value = turned if n == 0 else jnp.where(block == n, turned, value)
            low = m & 1
            out[0, 2 * pair + (m >> 1), :, low * LANES : (low + 1) * LANES] = value


def gather(came, before, at):
    _, nj, wide, width = before.shape
    return pl.pallas_call(
        functools.partial(gather_kernel, nj),
        out_shape=jax.ShapeDtypeStruct(before.shape, before.dtype),
        grid=(1,),
        in_specs=[
            pl.BlockSpec(came.shape, lambda i: (0,) * 6),
            pl.BlockSpec(memory_space=pl.ANY),
        ],
        out_specs=pl.BlockSpec((1, nj, wide, width), lambda i: (at, 0, 0, 0)),
        input_output_aliases={1: 0},
        compiler_params=pltpu.CompilerParams(vmem_limit_bytes=60 * 2**20),
        cost_estimate=pl.CostEstimate(flops=1000, bytes_accessed=1000, transcendentals=0),
        name="gather",
    )(came, before)


def tiled_body(amplitudes, integrals):
    ni, la, lk, full_c = amplitudes.shape
    z, x, core, row = (lax.axis_index(n) for n in ("z", "x", "core", "row"))
    place = jnp.stack([z, x, core]).astype(jnp.int32)
    amps = amplitudes.reshape(ni, la * lk, full_c)
    counts = CHUNKS
    starts = [sum(counts[:n]) for n in range(len(counts))]
    first = prep(amps, place, la, lk, 0, counts[0], (2, 3))
    integrals, *first = lax.optimization_barrier((integrals, *first))
    w_own = jnp.transpose(integrals, (0, 2, 1, 3))
    (next_place,) = gated((place,), w_own)
    parts = [first]
    for s, c in zip(starts[1:], counts[1:]):
        parts.append(prep(amps, next_place, la, lk, s, c, (2, 3)))
    moved = [(swapped(two, "z", 2), swapped(three, "z", 3)) for two, three in parts]
    w_x = swapped(w_own, "x")
    w_core = swapped(w_own, "core")
    (later,) = gated((place,), parts[0][0], parts[1][0], w_own)
    own, one = prep(amps, later, la, lk, 0, ni, (0, 1))
    one = swapped(one, "z", 1)
    (w_x,) = gated((w_x,), *moved[0], *moved[1], one, *[p[0] for p in parts[2:]])
    w_both = swapped(w_x, "core")
    ws = (w_own, w_core, w_x, w_both)

    where = [(m, i) for m, count in enumerate(counts) for i in range(count)]
    totals = []
    n = 0
    for g, count in enumerate(GROUPS):
        at = range(n, n + count)
        n += count
        two = [(moved[where[i][0]][0], where[i][1]) for i in at]
        three = [(moved[where[i][0]][1], where[i][1]) for i in at]
        totals.append(product(place, ([(own, i) for i in at], [(one, i) for i in at], two, three), ws, g >= CHAINED))

    def exchange(total, axis, mine, bits, *after):
        kept = lax.dynamic_index_in_dim(total, mine, 0, keepdims=False)
        sent = lax.dynamic_index_in_dim(total, 1 - mine, 0, keepdims=False)
        if after:
            (sent,) = gated((sent,), *after)
        if bits == 2:
            return kept + swapped(sent.astype(jnp.bfloat16), axis, bits).astype(jnp.float32)
        return kept + swapped(sent, axis, bits)

    result = None
    rows, lows, highs = [], [], []
    for g, total in enumerate(totals[:CHAINED]):
        rows.append(exchange(total, "row", row, 1, *rows[g - 1 : g], *lows[max(g - 2, 0) : max(g - 1, 0)]))
        lows.append(exchange(rows[g], "z", z & 1, 1, *lows[max(g - 1, 0) : g]))
        highs.append(exchange(lows[g], "z", z >> 1, 2))
    for g, total in enumerate(highs):
        pieces = [total]
        for bits in (1, 2, 3):
            pairs = [(s, s ^ bits) for s in range(4)]
            pieces.append(lax.ppermute(total, ("x", "core"), pairs))
        result = finish(place, pieces, sum(GROUPS[:g]), ni, result)
    for g, total in enumerate(totals[CHAINED:], CHAINED):
        came = total.reshape(32, -1, 32, LANES)
        came = lax.all_to_all(came, ("z", "x", "core", "row"), split_axis=0, concat_axis=0, tiled=True)
        result = gather(came.reshape(total.shape), result, sum(GROUPS[:g]))
    return jnp.transpose(result, (0, 3, 1, 2))


def solution(mesh):
    ta, rows = mesh.shape["ta"], mesh.shape["row"]

    def fn(amplitudes, integrals):
        ni, a, k, c = amplitudes.shape
        la, lk = a // ta, k // rows
        fits = ta == 16 and rows == 2 and c == 4 * LANES and la % 16 == 0 and lk % 8 == 0
        fits = fits and ni == sum(GROUPS)
        if not fits:
            placed = (P(None, "ta", "row", None), P("row", "ta", None, None))
            return jax.shard_map(
                gathered_body,
                mesh=mesh,
                in_specs=placed,
                out_specs=P(None, "row", None, "ta"),
                check_vma=False,
            )(amplitudes, integrals)
        fine = Mesh(mesh.devices.reshape(4, 2, 2, 2), ("z", "x", "core", "row"))
        ta_axes = ("z", "x", "core")
        return jax.shard_map(
            tiled_body,
            mesh=fine,
            in_specs=(P(None, ta_axes, "row", None), P("row", ta_axes, None, None)),
            out_specs=P(None, "row", None, ta_axes),
            check_vma=False,
        )(amplitudes, integrals)

    return fn
```
